128 devices in a mesh: pre: 8 (over x, core), dec: 16 (over z, y).
Axes of the slice: x: 4, y: 4, z: 4, core: 2. Of those that a mesh axis runs over, the one named last changes fastest.
Arguments:
- queries: bfloat16 [64, 128, 8192], P('pre', None, 'dec'), may hold values from -6 to 6, as said below
- branch_kv: bfloat16 [64, 128, 2048], P('pre', None, 'dec'), may hold values from -6 to 6
- pool_kv: bfloat16 [32, 128, 2048], P('pre', None, 'dec'), may hold values from -6 to 6, as said below
- page_lists: int32 [64, 16], replicated, may hold values from 0 to 31, as said below
- anc_len: int32 [64], replicated, may hold values from 1025 to 2048
- dec_owner: int32 [64], replicated, may hold values from 0 to 15, as said below
- output_projection_weight: bfloat16 [8192, 8192], P('dec'), may hold values from -0.0625 to 0.0625
Outputs:
- layer_out: bfloat16 [64, 128, 8192], P('pre', None, 'dec')
- decode_pages: bfloat16 [128, 128, 2048], P('dec', None, 'pre')
The draws below stay inside these ranges and needn't reach their ends.
Inputs may be any that keep to these rules, and one draw needn't show every extreme that they name: `queries`: floats within the range. `pool_kv`: floats within the range. `page_lists`: each branch lists distinct pages; the first half of the slots holds the same pages for every branch. `dec_owner`: the 8 branches of one prefill device (branches p * 8 on) go to distinct decode owners; one decode owner receives a branch from every prefill device.
All inputs are finite; a program needn't handle non-finite values.
Results may differ from the reference program's by a relative error of at most 0.024.
Values may be sent and summed in bfloat16 or wider, within the bound.
No kernel may reach another device: no remote copies, remote signals or barrier semaphores. Data moves between devices by JAX's collectives and lax.ppermute only.
A program may use at most 128 MiB of HBM per device.

```python
import jax
import jax.numpy as jnp
from jax import lax

D = 8192
QH = 64
KVH = 8
HD = 128
PAGE = 128
NANC = 16
BR_DEV = 8
BRANCHES = 64
NPAGES = 32
N_PRE = 8
N_DEC = 16


def draw_queries(key, part):
    own_key = jax.random.fold_in(key, 11)
    shape = (BRANCHES, PAGE, QH, HD)
    base = jnp.clip(jax.random.normal(own_key, shape, jnp.float32), -6.0, 6.0)
    return base.reshape(BRANCHES, PAGE, QH * HD).astype(jnp.bfloat16)


def draw_pool_kv(key, part):
    own_key = jax.random.fold_in(key, 12)
    shape = (NPAGES, PAGE, KVH, 2, HD)
    base = jnp.clip(jax.random.normal(own_key, shape, jnp.float32), -6.0, 6.0)
    return base.reshape(NPAGES, PAGE, 2 * KVH * HD).astype(jnp.bfloat16)


def draw_page_lists(key, part):
    base_key = jax.random.fold_in(key, 13)
    order = jax.random.permutation(base_key, NPAGES).astype(jnp.int32)
    shared = NANC // 2
    root = order[:shared]
    rest = order[shared:]
    branch_keys = jax.random.split(jax.random.fold_in(base_key, 1), BRANCHES)
    tails = jax.vmap(lambda k: jax.random.permutation(k, rest)[:NANC - shared])(branch_keys)
    heads = jnp.broadcast_to(root[None, :], (BRANCHES, shared))
    return jnp.concatenate([heads, tails], 1).astype(jnp.int32)


def draw_dec_owner(key, part):
    base_key = jax.random.fold_in(key, 14)
    hot = jax.random.randint(base_key, (), 0, N_DEC).astype(jnp.int32)
    row_keys = jax.random.split(jax.random.fold_in(base_key, 1), N_PRE)

    def one_row(row_key):
        first, second = jax.random.split(row_key)
        others = jax.random.permutation(first, N_DEC - 1).astype(jnp.int32)
        others = others + (others >= hot).astype(jnp.int32)
        chosen = jnp.concatenate([hot[None], others[:BR_DEV - 1]])
        return jax.random.permutation(second, chosen)
    return jax.vmap(one_row)(row_keys).reshape(BRANCHES).astype(jnp.int32)


def place_ends(values, rng, least, high):
    longest = values.shape.index(max(values.shape))
    spots = []
    for shift in (0, 1):
        where = [jax.random.randint(jax.random.fold_in(rng, axis), (), 0, length) for axis, length in enumerate(values.shape)]
        where[longest] = (where[longest] + shift) % values.shape[longest]
        spots.append(tuple(where))
    return values.at[spots[0]].set(least).at[spots[1]].set(high)


def steps_of(key, shape, pieces, least, high):
    def one(dim, parts):
        steps = jax.random.uniform(jax.random.fold_in(jax.random.fold_in(key, 6), dim), (parts,), jnp.float32, least / len(pieces), high / len(pieces))
        return jnp.repeat(jnp.exp(steps), shape[dim] // parts).reshape((-1,) + (1,) * (len(shape) - dim - 1))

    gain = one(*pieces[0])
    for cut in pieces[1:]:
        gain = gain * one(*cut)
    return gain


def gaussian(key, extent, deviation, limit, cuts=(), held_as=jnp.bfloat16):
    values = jax.random.normal(key, extent, jnp.float32) * deviation
    if len(cuts) > 0:
        values = steps_of(key, extent, cuts, -0.22, 0.18) * values
    return jnp.clip(values, min=-limit, max=limit).astype(held_as)


def setup_inputs(seed: int = 0) -> dict:
    seeds = jax.random.split(jax.random.key(seed), 8)
    queries = draw_queries(jax.random.fold_in(seeds[7], 71), 0)
    branch_kv = gaussian(seeds[1], (BRANCHES, PAGE, 2 * KVH * HD), 1.0, 6.0, ((0, 8), (2, 16)))
    pool_kv = draw_pool_kv(jax.random.fold_in(seeds[7], 71), 0)
    page_lists = draw_page_lists(jax.random.fold_in(seeds[7], 71), 0)
    anc_len = place_ends(jax.random.randint(seeds[4], (BRANCHES,), NANC // 2 * PAGE + 1, NANC * PAGE + 1), jax.random.fold_in(seeds[4], 1), NANC // 2 * PAGE + 1, NANC * PAGE).astype(jnp.int32)
    dec_owner = draw_dec_owner(jax.random.fold_in(seeds[7], 71), 0)
    output_projection_weight = gaussian(seeds[6], (QH * HD, D), (QH * HD) ** -0.5, 0.0625, ((0, 16),))
    return dict(queries=queries, branch_kv=branch_kv, pool_kv=pool_kv, page_lists=page_lists, anc_len=anc_len, dec_owner=dec_owner, output_projection_weight=output_projection_weight)


def reference(queries, branch_kv, pool_kv, page_lists, anc_len, dec_owner, output_projection_weight):
    group = QH // KVH
    softmax_scale = HD ** -0.5

    def one_branch(item):
        q_rows, own_rows, pages, count = item
        query_vectors = q_rows.reshape(PAGE, QH, HD).astype(jnp.float32)
        ancestors = pool_kv[pages.astype(jnp.int32)].reshape(NANC * PAGE, KVH, 2, HD)
        own = own_rows.reshape(PAGE, KVH, 2, HD)
        keys = jnp.concatenate([ancestors[:, :, 0], own[:, :, 0]], 0)
        values = jnp.concatenate([ancestors[:, :, 1], own[:, :, 1]], 0)
        keys = jnp.repeat(keys, group, axis=1).astype(jnp.float32)
        values = jnp.repeat(values, group, axis=1).astype(jnp.float32)
        scores = jnp.einsum("qhd,khd->qhk", query_vectors, keys) * softmax_scale
        position = jnp.arange(NANC * PAGE, dtype=jnp.int32)
        earlier = jnp.broadcast_to((position < count)[None, :], (PAGE, NANC * PAGE))
        causal = jnp.arange(PAGE, dtype=jnp.int32)[None, :] <= jnp.arange(PAGE, dtype=jnp.int32)[:, None]
        allowed = jnp.concatenate([earlier, causal], 1)
        scores = jnp.where(allowed[:, None, :], scores, -jnp.inf)
        top = jnp.max(scores, axis=-1, keepdims=True)
        weights = jnp.exp(scores - top)
        running_denominator = jnp.sum(weights, axis=-1)
        probs = lax.optimization_barrier(weights.astype(jnp.bfloat16)).astype(jnp.float32)
        out = jnp.einsum("qhk,khd->qhd", probs, values) / running_denominator[..., None]
        return out.reshape(PAGE, QH * HD).astype(jnp.bfloat16)

    attention_result = lax.map(one_branch, (queries, branch_kv, page_lists, anc_len))
    attn_flat = attention_result.reshape(BRANCHES * PAGE, QH * HD)
    width = QH * HD // N_DEC

    def add_group(index, running_denominator):
        start = (index * width).astype(jnp.int32)
        cols = lax.dynamic_slice_in_dim(attn_flat, start, width, 1)
        rows = lax.dynamic_slice_in_dim(output_projection_weight, start, width, 0)
        exponent_term = jnp.dot(cols, rows, preferred_element_type=jnp.float32)
        exponent_term = lax.optimization_barrier(exponent_term.astype(jnp.bfloat16)).astype(jnp.float32)
        return running_denominator + exponent_term

    summed = lax.fori_loop(0, N_DEC, add_group, jnp.zeros((BRANCHES * PAGE, D), jnp.float32))
    layer_out = summed.astype(jnp.bfloat16).reshape(BRANCHES, PAGE, D)

    owners = dec_owner.reshape(N_PRE, BR_DEV)
    onehot = (owners[:, :, None] == jnp.arange(N_DEC, dtype=jnp.int32)[None, None, :]).astype(jnp.float32)
    kv_rows = branch_kv.reshape(N_PRE, BR_DEV, PAGE, 2 * KVH * HD).astype(jnp.float32)
    placed = jnp.einsum("pbo,pbqc->opqc", onehot, kv_rows)
    decode_pages = placed.reshape(N_DEC * N_PRE, PAGE, 2 * KVH * HD).astype(jnp.bfloat16)
    return layer_out, decode_pages
```

```python
import functools

import jax
import jax.numpy as jnp
from jax import lax
from jax.experimental import pallas as pl
from jax.experimental.pallas import tpu as pltpu
from jax.sharding import PartitionSpec as P

HD = 128
PAGE = 128
LOG2E = 1.4426950408889634
MASKED = -1e30
N_X, N_CORE, N_Z, N_Y = 4, 2, 4, 4
N_PRE, N_DEC = N_X * N_CORE, N_Z * N_Y
ANY = pl.BlockSpec(memory_space=pl.ANY)
SMEM = pl.BlockSpec(memory_space=pltpu.SMEM)


def shift_pre(value, dx, dcore):
    pairs = []
    for p in range(N_PRE):
        x, core = divmod(p, N_CORE)
        pairs.append((p, (x + dx) % N_X * N_CORE + (core + dcore) % N_CORE))
    return lax.ppermute(value, "pre", pairs)


def shift_dec(value, dz, dy):
    pairs = []
    for d in range(N_DEC):
        z, y = divmod(d, N_Y)
        pairs.append((d, (z + dz) % N_Z * N_Y + (y + dy) % N_Y))
    return lax.ppermute(value, "dec", pairs)


def swap_pair(value):
    return lax.ppermute(value, "dec", [(d, d ^ 1) for d in range(N_DEC)])


def dot_nt(a, b):
    return lax.dot_general(a, b, (((1,), (1,)), ((), ())), preferred_element_type=jnp.float32)


def dot_nn(a, b):
    return lax.dot_general(a, b, (((1,), (0,)), ((), ())), preferred_element_type=jnp.float32)


def attention_kernel(
    first, heads, pages_ref, len_ref, where_ref, q_ref, mine_ref, other_ref, *rest
):
    pieces = rest[:8]
    out_ref, kv, s_ref, sems = rest[8:]
    branch = pl.program_id(0)

    @pl.when(branch == 0)
    def _():
        copies = [
            pltpu.make_async_copy(
                pieces[i], kv.at[:, pl.ds(where_ref[1 + i] * 4, 4)], sems.at[i]
            )
            for i in range(8)
        ]
        for copy in copies:
            copy.start()
        for copy in copies:
            copy.wait()

    key_kind = where_ref[0]
    value_kind = 1 - key_kind
    row = where_ref[9] + first + branch
    count = len_ref[row]
    scale = HD**-0.5 * LOG2E
    rows = heads * PAGE
    q = jnp.concatenate([q_ref[0, :, h * HD : (h + 1) * HD] for h in range(heads)], axis=0)

    def page_pair(kind, pair):
        parts = [kv[kind, pages_ref[row, 2 * pair + i]] for i in range(2)]
        return jnp.concatenate(parts, axis=0)

    peak = None
    for pair in range(8):
        s = dot_nt(q, page_pair(key_kind, pair)) * scale
        if pair >= 4:
            position = lax.broadcasted_iota(jnp.int32, (rows, 256), 1) + pair * 256
            s = jnp.where(position < count, s, MASKED)
        s_ref[:, pair * 256 : (pair + 1) * 256] = s
        top = jnp.maximum(s[:, :128], s[:, 128:])
        peak = top if peak is None else jnp.maximum(peak, top)
    mine_is_key = key_kind == 0
    mine, other = mine_ref[0], other_ref[0]
    own_keys = jnp.where(mine_is_key, mine, other)
    own_values = jnp.where(mine_is_key, other, mine)
    token = lax.broadcasted_iota(jnp.int32, (heads, PAGE, PAGE), 1).reshape(rows, PAGE)
    key = lax.broadcasted_iota(jnp.int32, (rows, PAGE), 1)
    s = jnp.where(key <= token, dot_nt(q, own_keys) * scale, MASKED)
    peak = jnp.max(jnp.maximum(peak, s), axis=1, keepdims=True)
    p = jnp.exp2(s - peak)
    total = p
    acc = dot_nn(p.astype(jnp.bfloat16), own_values)
    for pair in range(8):
        p = jnp.exp2(s_ref[:, pair * 256 : (pair + 1) * 256] - peak)
        total = total + p[:, :128] + p[:, 128:]
        acc = acc + dot_nn(p.astype(jnp.bfloat16), page_pair(value_kind, pair))
    out = acc / jnp.sum(total, axis=1, keepdims=True)
    for h in range(heads):
        out_ref[0, :, h * HD : (h + 1) * HD] = out[h * PAGE : (h + 1) * PAGE].astype(out_ref.dtype)


def attention(q, mine, other, pieces, pages, lens, where, first, count):
    cols = q.shape[2]
    heads = cols // HD
    grid_spec = pltpu.PrefetchScalarGridSpec(
        num_scalar_prefetch=3,
        grid=(count,),
        in_specs=[
            pl.BlockSpec((1, PAGE, cols), lambda b, *_: (first + b, 0, 0)),
            pl.BlockSpec((1, PAGE, HD), lambda b, *_: (first + b, 0, 0)),
            pl.BlockSpec((1, PAGE, HD), lambda b, *_: (first + b, 0, 0)),
        ]
        + [ANY] * 8,
        out_specs=pl.BlockSpec((1, PAGE, cols), lambda b, *_: (b, 0, 0)),
        scratch_shapes=[
            pltpu.VMEM((2, 32, PAGE, HD), jnp.bfloat16),
            pltpu.VMEM((heads * PAGE, 2048), jnp.float32),
            pltpu.SemaphoreType.DMA((8,)),
        ],
    )
    work = count * heads * PAGE * 2176
    return pl.pallas_call(
        functools.partial(attention_kernel, first, heads),
        grid_spec=grid_spec,
        out_shape=jax.ShapeDtypeStruct((count, PAGE, cols), jnp.bfloat16),
        compiler_params=pltpu.CompilerParams(vmem_limit_bytes=40 << 20),
        cost_estimate=pl.CostEstimate(
            flops=work * 128 * 4 * 2, bytes_accessed=4 << 20, transcendentals=work
        ),
    )(pages, lens, where, q, mine, other, *pieces)


def weight_pieces_kernel(where_ref, w_ref, one_ref, two_ref, three_ref, sems):
    pre, y = where_ref[0], where_ref[1]
    copies = []
    for s, out_ref in ((1, one_ref), (2, two_ref), (3, three_ref)):
        col = lax.rem(y + s, N_Y)
        for z in range(N_Z):
            copies.append(
                pltpu.make_async_copy(
                    w_ref.at[pl.ds(pre * 64, 64), pl.ds((z * N_Y + col) * 512, 512)],
                    out_ref.at[z],
                    sems.at[s - 1, z],
                )
            )
    for copy in copies:
        copy.start()
    for copy in copies:
        copy.wait()


def weight_pieces(where, weight):
    shape = jax.ShapeDtypeStruct((N_Z, 64, 512), jnp.bfloat16)
    return pl.pallas_call(
        weight_pieces_kernel,
        in_specs=[SMEM, ANY],
        out_specs=[ANY] * 3,
        out_shape=[shape] * 3,
        scratch_shapes=[pltpu.SemaphoreType.DMA((3, N_Z))],
        cost_estimate=pl.CostEstimate(flops=0, bytes_accessed=3 << 19, transcendentals=0),
    )(where, weight)


def project_kernel(where_ref, a0, a1, a2, a3, w0, w1, w2, w3, o0, o1, o2, o3):
    step = pl.program_id(0)
    acc = dot_nn(a0[...], w0[...])
    for a, w in ((a1, w1), (a2, w2), (a3, w3)):
        acc = acc + dot_nn(a[...], w[...].reshape(512, 512))
    for s, out in ((1, o1), (2, o2), (3, o3)):

        @pl.when(step == s - 1)
        def _():
            out[...] = acc.astype(jnp.bfloat16)

    @pl.when(step == 3)
    def _():
        o0[...] = acc


def project(where, pieces, weight, gathered):
    rows = pieces[0].shape[0]

    def column(i, w):
        return lax.rem(w[2] + i + 1, N_Z)

    full = pl.BlockSpec((rows, 512), lambda i, w: (0, 0))
    grid_spec = pltpu.PrefetchScalarGridSpec(
        num_scalar_prefetch=1,
        grid=(4,),
        in_specs=[full] * 4
        + [pl.BlockSpec((512, 512), lambda i, w: (0, column(i, w) * N_Y + w[1]))]
        + [
            pl.BlockSpec(
                (N_PRE, 1, 1, 64, 512), lambda i, w, s=s: (0, s, column(i, w), 0, 0)
            )
            for s in range(3)
        ],
        out_specs=[full] * 4,
        scratch_shapes=[],
    )
    shapes = [jax.ShapeDtypeStruct((rows, 512), jnp.float32)]
    shapes += [jax.ShapeDtypeStruct((rows, 512), jnp.bfloat16)] * 3
    return pl.pallas_call(
        project_kernel,
        grid_spec=grid_spec,
        out_shape=shapes,
        compiler_params=pltpu.CompilerParams(vmem_limit_bytes=40 << 20),
        cost_estimate=pl.CostEstimate(
            flops=2 * rows * 2048 * 2048, bytes_accessed=16 << 20, transcendentals=0
        ),
    )(where, *pieces, weight, gathered, gathered, gathered)


def on_device(
    queries, branch_kv, pool_kv, page_lists, anc_len, dec_owner, output_projection_weight
):
    pre_idx = lax.axis_index("pre")
    dec_idx = lax.axis_index("dec")
    branch_count, page_len, cols = queries.shape
    x, core = pre_idx // N_CORE, pre_idx % N_CORE
    z, y = dec_idx // N_Y, dec_idx % N_Y
    place = jnp.stack([pre_idx, y, z]).astype(jnp.int32)

    other_pool = swap_pair(pool_kv)
    w1, w2, w3 = weight_pieces(place, output_projection_weight)
    other_own = swap_pair(branch_kv)
    both = jnp.stack([pool_kv, other_pool])
    by_shift = [both] + [shift_pre(both, s, 0) for s in (1, 3, 2)]
    swapped = [shift_pre(piece, 0, 1) for piece in by_shift]
    spots = [(x + N_X - s) % N_X * N_CORE + core for s in (0, 1, 3, 2)]
    spots += [(x + N_X - s) % N_X * N_CORE + (1 - core) for s in (0, 1, 3, 2)]
    where = jnp.stack([dec_idx % 2] + spots + [pre_idx * branch_count]).astype(jnp.int32)

    received = [shift_dec(w, 0, s) for s, w in ((1, w1), (2, w2), (3, w3))]
    gathered = lax.all_gather(jnp.stack(received), "pre", axis=0)

    half = branch_count // 2
    outs = []
    for first in range(0, branch_count, half):
        attn = attention(
            queries, branch_kv, other_own, by_shift + swapped, page_lists, anc_len, where, first, half
        ).reshape(half * page_len, cols)
        pieces = [attn] + [shift_dec(attn, 0, s) for s in (1, 2, 3)]
        terms = project(place, pieces, output_projection_weight, gathered)
        arrived = [shift_dec(terms[s], s, 0) for s in (1, 2, 3)]
        total = terms[0]
        for part in arrived:
            total = total + part.astype(jnp.float32)
        outs.append(total.astype(jnp.bfloat16).reshape(half, page_len, 512))
    layer_out = jnp.concatenate(outs, axis=0)

    owners = lax.dynamic_slice_in_dim(dec_owner, pre_idx * branch_count, branch_count, 0)
    pairs = [
        (p * N_DEC + d, d // 2 * N_DEC + 2 * p + d % 2) for p in range(N_PRE) for d in range(N_DEC)
    ]
    turned = lax.ppermute(branch_kv, ("pre", "dec"), pairs)
    from_pre = dec_idx // 2
    owners = lax.dynamic_slice_in_dim(dec_owner, from_pre * branch_count, branch_count, 0)
    onehot = (owners[None, :] == jnp.arange(N_DEC, dtype=jnp.int32)[:, None]).astype(jnp.bfloat16)
    buckets = jnp.einsum(
        "ob,bqc->oqc", onehot, turned, preferred_element_type=jnp.float32
    ).astype(jnp.bfloat16)
    buckets, _ = lax.optimization_barrier((buckets, terms[1]))
    moved = lax.all_to_all(buckets, "dec", split_axis=0, concat_axis=0, tiled=True)
    moved = moved.reshape(N_PRE, 2, page_len, HD).transpose(0, 2, 1, 3)
    decode_pages = moved.reshape(N_PRE, page_len, 2 * HD)
    return (layer_out, decode_pages)


def solution(mesh):
    in_specs = (
        P("pre", None, "dec"),
        P("pre", None, "dec"),
        P("pre", None, "dec"),
        P(),
        P(),
        P(),
        P("dec", None),
    )
    out_specs = (P("pre", None, "dec"), P("dec", None, "pre"))
    return jax.shard_map(
        on_device, mesh=mesh, in_specs=in_specs, out_specs=out_specs, check_vma=False
    )
```

```python
import functools

import jax
import jax.numpy as jnp
import numpy as np
from jax import lax
from jax.experimental import pallas as pl
from jax.experimental.pallas import tpu as pltpu
from jax.sharding import PartitionSpec as P

HD = 128
PAGE = 128
LOG2E = 1.4426950408889634
MASKED = -1e30
N_X, N_CORE, N_Z, N_Y = 4, 2, 4, 4
N_PRE, N_DEC = N_X * N_CORE, N_Z * N_Y
VMEM_LIMIT = 60 << 20
PRE_AT, Y_AT, Z_AT = 10, 11, 12
ANY = pl.BlockSpec(memory_space=pl.ANY)
SMEM = pl.BlockSpec(memory_space=pltpu.SMEM)


def shift_pre(value, dx, dcore):
    pairs = []
    for p in range(N_PRE):
        x, core = divmod(p, N_CORE)
        pairs.append((p, (x + dx) % N_X * N_CORE + (core + dcore) % N_CORE))
    return lax.ppermute(value, "pre", pairs)


def shift_dec(value, dz, dy):
    pairs = []
    for d in range(N_DEC):
        z, y = divmod(d, N_Y)
        pairs.append((d, (z + dz) % N_Z * N_Y + (y + dy) % N_Y))
    return lax.ppermute(value, "dec", pairs)


def swap_pair(value):
    return lax.ppermute(value, "dec", [(d, d ^ 1) for d in range(N_DEC)])


def dot_nt(a, b):
    return lax.dot_general(a, b, (((1,), (1,)), ((), ())), preferred_element_type=jnp.float32)


def dot_nn(a, b):
    return lax.dot_general(a, b, (((1,), (0,)), ((), ())), preferred_element_type=jnp.float32)


def attention_kernel(
    first, heads, pages_ref, len_ref, where_ref, q_ref, mine_ref, other_ref, *rest
):
    pieces = rest[:8]
    out_ref, kv, s_ref, sems = rest[-4:]
    branch = pl.program_id(0)

    @pl.when(branch == 0)
    def _():
        copies = [
            pltpu.make_async_copy(
                pieces[i], kv.at[:, pl.ds(where_ref[1 + i] * 4, 4)], sems.at[i]
            )
            for i in range(8)
        ]
        for copy in copies:
            copy.start()
        for copy in copies:
            copy.wait()

    key_kind = where_ref[0]
    value_kind = 1 - key_kind
    row = where_ref[9] + first + branch
    count = len_ref[row]
    scale = HD**-0.5 * LOG2E
    rows = heads * PAGE
    q = jnp.concatenate([q_ref[0, :, h * HD : (h + 1) * HD] for h in range(heads)], axis=0)

    def page_pair(kind, pair):
        parts = [kv[kind, pages_ref[row, 2 * pair + i]] for i in range(2)]
        return jnp.concatenate(parts, axis=0)

    peak = None
    for pair in range(8):
        s = dot_nt(q, page_pair(key_kind, pair)) * scale
        if pair >= 4:
            position = lax.broadcasted_iota(jnp.int32, (rows, 256), 1) + pair * 256
            s = jnp.where(position < count, s, MASKED)
        s_ref[:, pair * 256 : (pair + 1) * 256] = s
        top = jnp.maximum(s[:, :128], s[:, 128:])
        peak = top if peak is None else jnp.maximum(peak, top)
    mine_is_key = key_kind == 0
    mine, other = mine_ref[0], other_ref[0]
    own_keys = jnp.where(mine_is_key, mine, other)
    own_values = jnp.where(mine_is_key, other, mine)
    token = lax.broadcasted_iota(jnp.int32, (heads, PAGE, PAGE), 1).reshape(rows, PAGE)
    key = lax.broadcasted_iota(jnp.int32, (rows, PAGE), 1)
    s = jnp.where(key <= token, dot_nt(q, own_keys) * scale, MASKED)
    peak = jnp.max(jnp.maximum(peak, s), axis=1, keepdims=True)
    p = jnp.exp2(s - peak)
    total = p
    acc = dot_nn(p.astype(jnp.bfloat16), own_values)
    for pair in range(8):
        p = jnp.exp2(s_ref[:, pair * 256 : (pair + 1) * 256] - peak)
        total = total + p[:, :128] + p[:, 128:]
        acc = acc + dot_nn(p.astype(jnp.bfloat16), page_pair(value_kind, pair))
    out = acc / jnp.sum(total, axis=1, keepdims=True)
    for h in range(heads):
        out_ref[0, :, h * HD : (h + 1) * HD] = out[h * PAGE : (h + 1) * PAGE].astype(out_ref.dtype)


def attention(q, mine, other, pieces, pages, lens, where, first, count, after=()):
    cols = q.shape[2]
    heads = cols // HD
    grid_spec = pltpu.PrefetchScalarGridSpec(
        num_scalar_prefetch=3,
        grid=(count,),
        in_specs=[
            pl.BlockSpec((1, PAGE, cols), lambda b, *_: (first + b, 0, 0)),
            pl.BlockSpec((1, PAGE, HD), lambda b, *_: (first + b, 0, 0)),
            pl.BlockSpec((1, PAGE, HD), lambda b, *_: (first + b, 0, 0)),
        ]
        + [ANY] * (8 + len(after)),
        out_specs=pl.BlockSpec((1, PAGE, cols), lambda b, *_: (b, 0, 0)),
        scratch_shapes=[
            pltpu.VMEM((2, 32, PAGE, HD), jnp.bfloat16),
            pltpu.VMEM((heads * PAGE, 2048), jnp.float32),
            pltpu.SemaphoreType.DMA((8,)),
        ],
    )
    work = count * heads * PAGE * 2176
    return pl.pallas_call(
        functools.partial(attention_kernel, first, heads),
        grid_spec=grid_spec,
        out_shape=jax.ShapeDtypeStruct((count, PAGE, cols), jnp.bfloat16),
        compiler_params=pltpu.CompilerParams(vmem_limit_bytes=VMEM_LIMIT),
        cost_estimate=pl.CostEstimate(
            flops=work * 128 * 4 * 2, bytes_accessed=4 << 20, transcendentals=work
        ),
    )(pages, lens, where, q, mine, other, *pieces, *after)


def weight_pieces_kernel(place_ref, w_ref, one_ref, two_ref, three_ref, sems):
    pre, y = place_ref[PRE_AT], place_ref[Y_AT]
    copies = []
    for s, out_ref in ((1, one_ref), (2, two_ref), (3, three_ref)):
        col = lax.rem(y + s, N_Y)
        for z in range(N_Z):
            copies.append(
                pltpu.make_async_copy(
                    w_ref.at[pl.ds(pre * 64, 64), pl.ds((z * N_Y + col) * 512, 512)],
                    out_ref.at[z],
                    sems.at[s - 1, z],
                )
            )
    for copy in copies:
        copy.start()
    for copy in copies:
        copy.wait()


def weight_pieces(place, weight):
    shape = jax.ShapeDtypeStruct((N_Z, 64, 512), jnp.bfloat16)
    return pl.pallas_call(
        weight_pieces_kernel,
        in_specs=[SMEM, ANY],
        out_specs=[pl.BlockSpec(memory_space=pltpu.VMEM)] * 3,
        out_shape=[shape] * 3,
        scratch_shapes=[pltpu.SemaphoreType.DMA((3, N_Z))],
        compiler_params=pltpu.CompilerParams(vmem_limit_bytes=VMEM_LIMIT),
        cost_estimate=pl.CostEstimate(flops=0, bytes_accessed=3 << 19, transcendentals=0),
    )(place, weight)


def project_kernel(place_ref, a0, a1, a2, a3, w0, w1, w2, w3, *rest):
    o0, o1, o2, o3 = rest[-4:]
    step = pl.program_id(0)
    acc = dot_nn(a0[...], w0[...])
    for a, w in ((a1, w1), (a2, w2), (a3, w3)):
        acc = acc + dot_nn(a[...], w[...].reshape(512, 512))
    for s, out in ((1, o1), (2, o2), (3, o3)):

        @pl.when(step == s - 1)
        def _():
            out[...] = acc.astype(jnp.bfloat16)

    @pl.when(step == 3)
    def _():
        o0[...] = acc


def project(place, attn, weight, gathered, after=()):
    rows = attn[0].shape[0]

    def column(i, w):
        return lax.rem(w[Z_AT] + i + 1, N_Z)

    full = pl.BlockSpec((rows, 512), lambda i, w: (0, 0))
    grid_spec = pltpu.PrefetchScalarGridSpec(
        num_scalar_prefetch=1,
        grid=(4,),
        in_specs=[full] * 4
        + [pl.BlockSpec((512, 512), lambda i, w: (0, column(i, w) * N_Y + w[Y_AT]))]
        + [
            pl.BlockSpec((N_PRE, 1, 1, 64, 512), lambda i, w, s=s: (0, s, column(i, w), 0, 0))
            for s in range(3)
        ]
        + [ANY] * len(after),
        out_specs=[full] * 4,
        scratch_shapes=[],
    )
    shapes = [jax.ShapeDtypeStruct((rows, 512), jnp.float32)]
    shapes += [jax.ShapeDtypeStruct((rows, 512), jnp.bfloat16)] * 3
    return pl.pallas_call(
        project_kernel,
        grid_spec=grid_spec,
        out_shape=shapes,
        compiler_params=pltpu.CompilerParams(vmem_limit_bytes=VMEM_LIMIT),
        cost_estimate=pl.CostEstimate(
            flops=2 * rows * 2048 * 2048, bytes_accessed=16 << 20, transcendentals=0
        ),
    )(place, *attn, weight, gathered, gathered, gathered, *after)


def bucket_kernel(owner_ref, pages_ref, _, out_ref):
    out_ref[...] = jnp.zeros_like(out_ref)
    for b in range(pages_ref.shape[0]):
        out_ref[owner_ref[b]] = pages_ref[b]


def bucket_pages(owners, pages, after):
    vmem = pl.BlockSpec(memory_space=pltpu.VMEM)
    return pl.pallas_call(
        bucket_kernel,
        in_specs=[SMEM, vmem, ANY],
        out_specs=vmem,
        out_shape=jax.ShapeDtypeStruct((N_DEC,) + pages.shape[1:], pages.dtype),
        compiler_params=pltpu.CompilerParams(vmem_limit_bytes=VMEM_LIMIT),
        cost_estimate=pl.CostEstimate(flops=0, bytes_accessed=3 << 18, transcendentals=0),
    )(owners, pages, after)


def stack_kernel(a_ref, b_ref, c_ref, *rest):
    out_ref = rest[-1]
    for i, ref in enumerate((a_ref, b_ref, c_ref)):
        out_ref[i] = ref[...]


def stack_after(parts, after):
    vmem = pl.BlockSpec(memory_space=pltpu.VMEM)
    return pl.pallas_call(
        stack_kernel,
        in_specs=[vmem] * 3 + [ANY] * len(after),
        out_specs=vmem,
        out_shape=jax.ShapeDtypeStruct((3,) + parts[0].shape, parts[0].dtype),
        cost_estimate=pl.CostEstimate(flops=0, bytes_accessed=3 << 19, transcendentals=0),
    )(*parts, *after)


def place_table():
    rows = []
    for p in range(N_PRE):
        for d in range(N_DEC):
            x, core = divmod(p, N_CORE)
            z, y = divmod(d, N_Y)
            spots = [(x - s) % N_X * N_CORE + c for c in (core, 1 - core) for s in (0, 1, 3, 2)]
            rows.append([d % 2] + spots + [p * 8, p, y, z])
    return np.array(rows, np.int32)


def on_device(
    queries, branch_kv, pool_kv, page_lists, anc_len, dec_owner, output_projection_weight
):
    pre_idx = lax.axis_index("pre")
    dec_idx = lax.axis_index("dec")
    branch_count, page_len, cols = queries.shape
    table = jnp.asarray(place_table())
    place = lax.dynamic_index_in_dim(table, pre_idx * N_DEC + dec_idx, keepdims=False)

    other_pool = swap_pair(pool_kv)
    both = jnp.stack([pool_kv, other_pool])
    other_own = swap_pair(branch_kv)
    by_shift = [both] + [shift_pre(both, s, 0) for s in (1, 3, 2)]
    swapped = [shift_pre(piece, 0, 1) for piece in by_shift]

    sent = weight_pieces(place, output_projection_weight)
    received = [shift_dec(w, 0, s) for s, w in zip((1, 2, 3), sent)]
    gathered = lax.all_gather(stack_after(received, by_shift[1:]), "pre", axis=0)

    half = branch_count // 2
    kv = by_shift + swapped

    def attend(first, after=()):
        attn = attention(
            queries, branch_kv, other_own, kv, page_lists, anc_len, place, first, half, after
        ).reshape(half * page_len, cols)
        return [attn] + [shift_dec(attn, 0, s) for s in (1, 2, 3)]

    def product(attn, after=()):
        terms = project(place, attn, output_projection_weight, gathered, after)
        arrived = [shift_dec(terms[s], s, 0) for s in (1, 2, 3)]
        total = terms[0]
        for part in arrived:
            total = total + part.astype(jnp.float32)
        return total.astype(jnp.bfloat16).reshape(half, page_len, 512)

    owners = lax.dynamic_slice_in_dim(dec_owner, pre_idx * branch_count, branch_count, 0)
    buckets = bucket_pages(owners, branch_kv, by_shift[3])
    owned = lax.all_to_all(buckets, "dec", split_axis=0, concat_axis=0, tiled=True)

    one = attend(0)
    two = attend(half, (owned,))
    moved = lax.all_to_all(owned, "pre", split_axis=0, concat_axis=0, tiled=True)

    layer_out = jnp.concatenate([product(one), product(two, (moved,))], axis=0)
    moved = moved.reshape(N_PRE, 2, page_len, HD).transpose(0, 2, 1, 3)
    decode_pages = moved.reshape(N_PRE, page_len, 2 * HD)
    return (layer_out, decode_pages)


def solution(mesh):
    in_specs = (
        P("pre", None, "dec"),
        P("pre", None, "dec"),
        P("pre", None, "dec"),
        P(),
        P(),
        P(),
        P("dec", None),
    )
    out_specs = (P("pre", None, "dec"), P("dec", None, "pre"))
    return jax.shard_map(
        on_device, mesh=mesh, in_specs=in_specs, out_specs=out_specs, check_vma=False
    )
```

```python
import functools

import jax
import jax.numpy as jnp
import numpy as np
from jax import lax
from jax.experimental import pallas as pl
from jax.experimental.pallas import tpu as pltpu
from jax.sharding import PartitionSpec as P

HD = 128
PAGE = 128
NANC = 16
ANCESTORS = NANC * PAGE
KEYS = ANCESTORS + PAGE
LOG2E = 1.4426950408889634
MASKED = -1e30
N_X, N_CORE, N_Z, N_Y = 4, 2, 4, 4
N_PRE, N_DEC = N_X * N_CORE, N_Z * N_Y
VMEM_LIMIT = 60 << 20
COST = 1 << 36
FIRST = 4
PRE_AT, Y_AT, Z_AT, ODD_AT, ROW_AT = range(5)
ANY = pl.BlockSpec(memory_space=pl.ANY)
SMEM = pl.BlockSpec(memory_space=pltpu.SMEM)


def shift_pre(value, dx, dcore):
    pairs = []
    for p in range(N_PRE):
        x, core = divmod(p, N_CORE)
        pairs.append((p, (x + dx) % N_X * N_CORE + (core + dcore) % N_CORE))
    return lax.ppermute(value, "pre", pairs)


def shift_dec(value, dz, dy):
    pairs = []
    for d in range(N_DEC):
        z, y = divmod(d, N_Y)
        pairs.append((d, (z + dz) % N_Z * N_Y + (y + dy) % N_Y))
    return lax.ppermute(value, "dec", pairs)


def swap_pair(value):
    return lax.ppermute(value, "dec", [(d, d ^ 1) for d in range(N_DEC)])


def dot_nt(a, b):
    return lax.dot_general(a, b, (((1,), (1,)), ((), ())), preferred_element_type=jnp.float32)


def dot_nn(a, b):
    return lax.dot_general(a, b, (((1,), (0,)), ((), ())), preferred_element_type=jnp.float32)


def attention_kernel(
    first, heads, pages_ref, len_ref, place_ref, q_ref, mine_ref, other_ref, kv_ref, *rest
):
    out_ref, kv, s_ref, k_all, v_all, sem = rest[-6:]
    odd = place_ref[ODD_AT]
    row = place_ref[ROW_AT] + first + pl.program_id(0)

    def load(slots):
        for slot in slots:
            page = pages_ref[row, slot]
            k_all[slot * PAGE : (slot + 1) * PAGE] = kv[page >> 2, odd, page & 3]
            v_all[slot * PAGE : (slot + 1) * PAGE, :HD] = kv[page >> 2, 1 - odd, page & 3]

    @pl.when(pl.program_id(0) == 0)
    def _():
        copy = pltpu.make_async_copy(kv_ref, kv, sem)
        copy.start()
        v_all[:, HD:] = jnp.ones((KEYS, HD), jnp.bfloat16)
        copy.wait()
        load(range(NANC // 2))

    load(range(NANC // 2, NANC))
    mine_is_key = odd == 0
    mine, other = mine_ref[0], other_ref[0]
    k_all[ANCESTORS:] = jnp.where(mine_is_key, mine, other)
    v_all[ANCESTORS:, :HD] = jnp.where(mine_is_key, other, mine)

    count = len_ref[row]
    scale = HD**-0.5 * LOG2E
    rows = 2 * PAGE
    for tile in range(heads // 2):
        here = slice(tile * rows, (tile + 1) * rows)
        lanes = [slice(h * HD, (h + 1) * HD) for h in (2 * tile, 2 * tile + 1)]
        q = jnp.concatenate([q_ref[0, :, cols] for cols in lanes], axis=0)
        token = lax.broadcasted_iota(jnp.int32, (2, PAGE, PAGE), 1).reshape(rows, PAGE)
        key = lax.broadcasted_iota(jnp.int32, (rows, PAGE), 1)
        own = jnp.where(key <= token, dot_nt(q, k_all[ANCESTORS:]), MASKED)
        peak = own
        for low in range(0, ANCESTORS, 256):
            s = dot_nt(q, k_all[low : low + 256])
            if low >= ANCESTORS // 2:
                position = lax.broadcasted_iota(jnp.int32, (1, 256), 1) + low
                s = s + jnp.where(position < count, 0.0, MASKED)
            s_ref[here, low : low + 256] = s
            peak = jnp.maximum(peak, jnp.maximum(s[:, :128], s[:, 128:]))
        peak = jnp.max(peak, axis=1, keepdims=True) * scale
        probs = [
            jnp.exp2(s_ref[here, low : low + 256] * scale - peak).astype(jnp.bfloat16)
            for low in range(0, ANCESTORS, 256)
        ]
        probs.append(jnp.exp2(own * scale - peak).astype(jnp.bfloat16))
        acc = dot_nn(jnp.concatenate(probs, axis=1), v_all[...])
        out = (acc[:, :HD] / acc[:, HD:]).astype(out_ref.dtype)
        for i, cols in enumerate(lanes):
            out_ref[0, :, cols] = out[i * PAGE : (i + 1) * PAGE]


def attention(q, mine, other, kv, pages, lens, place, first, count, after=()):
    cols = q.shape[2]
    heads = cols // HD
    grid_spec = pltpu.PrefetchScalarGridSpec(
        num_scalar_prefetch=3,
        grid=(count,),
        in_specs=[
            pl.BlockSpec((1, PAGE, cols), lambda b, *_: (first + b, 0, 0)),
            pl.BlockSpec((1, PAGE, HD), lambda b, *_: (first + b, 0, 0)),
            pl.BlockSpec((1, PAGE, HD), lambda b, *_: (first + b, 0, 0)),
        ]
        + [ANY] * (1 + len(after)),
        out_specs=pl.BlockSpec((1, PAGE, cols), lambda b, *_: (b, 0, 0)),
        scratch_shapes=[
            pltpu.VMEM((N_PRE, 2, 4, PAGE, HD), jnp.bfloat16),
            pltpu.VMEM((heads * PAGE, ANCESTORS), jnp.float32),
            pltpu.VMEM((KEYS, HD), jnp.bfloat16),
            pltpu.VMEM((KEYS, 2 * HD), jnp.bfloat16),
            pltpu.SemaphoreType.DMA,
        ],
    )
    work = count * heads * PAGE * KEYS
    return pl.pallas_call(
        functools.partial(attention_kernel, first, heads),
        grid_spec=grid_spec,
        out_shape=jax.ShapeDtypeStruct((count, PAGE, cols), jnp.bfloat16),
        compiler_params=pltpu.CompilerParams(vmem_limit_bytes=VMEM_LIMIT),
        cost_estimate=pl.CostEstimate(
            flops=work * 128 * 4 * 2, bytes_accessed=4 << 20, transcendentals=work
        ),
    )(pages, lens, place, q, mine, other, kv, *after)


def weight_pieces_kernel(place_ref, w_ref, _, one_ref, two_ref, three_ref, sems):
    pre, y = place_ref[PRE_AT], place_ref[Y_AT]
    copies = []
    for s, out_ref in ((1, one_ref), (2, two_ref), (3, three_ref)):
        col = lax.rem(y + s, N_Y)
        for z in range(N_Z):
            copies.append(
                pltpu.make_async_copy(
                    w_ref.at[pl.ds(pre * 64, 64), pl.ds((z * N_Y + col) * 512, 512)],
                    out_ref.at[z],
                    sems.at[s - 1, z],
                )
            )
    for copy in copies:
        copy.start()
    for copy in copies:
        copy.wait()


def weight_pieces(place, weight, after):
    shape = jax.ShapeDtypeStruct((N_Z, 64, 512), jnp.bfloat16)
    return pl.pallas_call(
        weight_pieces_kernel,
        in_specs=[SMEM, ANY, ANY],
        out_specs=[pl.BlockSpec(memory_space=pltpu.VMEM)] * 3,
        out_shape=[shape] * 3,
        scratch_shapes=[pltpu.SemaphoreType.DMA((3, N_Z))],
        compiler_params=pltpu.CompilerParams(vmem_limit_bytes=VMEM_LIMIT),
        cost_estimate=pl.CostEstimate(flops=0, bytes_accessed=3 << 19, transcendentals=0),
    )(place, weight, after)


def project_body(steps, place_ref, a0, a1, a2, a3, w0, w1, w2, w3, *rest):
    acc = dot_nn(a0[...], w0[...])
    for a, w in ((a1, w1), (a2, w2), (a3, w3)):
        acc = acc + dot_nn(a[...], w[...].reshape(512, 512))
    for step, out in enumerate(rest[-steps:]):

        @pl.when(pl.program_id(0) == step)
        def _():
            out[...] = acc.astype(out.dtype)


def project(far, place, attn, weight, gathered, cost, after=()):
    rows = attn[0].shape[0] // (2 if far else 1)
    steps = 2 if far else 3

    def column(i, w):
        return lax.rem(w[Z_AT] + (2 if far else 1 + i + jnp.minimum(i, 1)), N_Z)

    def here(i, w):
        return (i if far else 0, 0)

    out = pl.BlockSpec((rows, 512), lambda i, w: (0, 0))
    grid_spec = pltpu.PrefetchScalarGridSpec(
        num_scalar_prefetch=1,
        grid=(steps,),
        in_specs=[pl.BlockSpec((rows, 512), here)] * 4
        + [pl.BlockSpec((512, 512), lambda i, w: (0, column(i, w) * N_Y + w[Y_AT]))]
        + [
            pl.BlockSpec((N_PRE, 1, 1, 64, 512), lambda i, w, s=s: (0, s, column(i, w), 0, 0))
            for s in range(3)
        ]
        + [ANY] * len(after),
        out_specs=[out] * steps,
        scratch_shapes=[],
    )
    kinds = [jnp.bfloat16] * 2 + [jnp.float32] * (steps - 2)
    return pl.pallas_call(
        functools.partial(project_body, steps),
        grid_spec=grid_spec,
        out_shape=[jax.ShapeDtypeStruct((rows, 512), kind) for kind in kinds],
        compiler_params=pltpu.CompilerParams(vmem_limit_bytes=VMEM_LIMIT),
        cost_estimate=pl.CostEstimate(flops=cost, bytes_accessed=cost >> 4, transcendentals=0),
    )(place, *attn, weight, gathered, gathered, gathered, *after)


def relay_kernel(next_ref, last_ref, low_ref, high_ref, next_out, last_out):
    half = low_ref.shape[0]
    up = next_ref[:half].astype(jnp.float32) + low_ref[...].astype(jnp.float32)
    next_out[:half] = up.astype(jnp.bfloat16)
    next_out[half:] = next_ref[half:]
    down = last_ref[half:].astype(jnp.float32) + high_ref[...].astype(jnp.float32)
    last_out[half:] = down.astype(jnp.bfloat16)
    last_out[:half] = last_ref[:half]


def relay(to_next, to_last, low, high):
    vmem = pl.BlockSpec(memory_space=pltpu.VMEM)
    return pl.pallas_call(
        relay_kernel,
        in_specs=[vmem] * 4,
        out_specs=[vmem] * 2,
        out_shape=[jax.ShapeDtypeStruct(to_next.shape, to_next.dtype)] * 2,
        cost_estimate=pl.CostEstimate(flops=1 << 20, bytes_accessed=3 << 20, transcendentals=0),
    )(to_next, to_last, low, high)


def copy_kernel(src_ref, _, out_ref):
    out_ref[...] = src_ref[...]


def copy_after(value, after):
    vmem = pl.BlockSpec(memory_space=pltpu.VMEM)
    return pl.pallas_call(
        copy_kernel,
        in_specs=[vmem, ANY],
        out_specs=vmem,
        out_shape=jax.ShapeDtypeStruct(value.shape, value.dtype),
        cost_estimate=pl.CostEstimate(flops=0, bytes_accessed=1 << 20, transcendentals=0),
    )(value, after)


def bucket_kernel(owner_ref, pages_ref, _, out_ref):
    out_ref[...] = jnp.zeros_like(out_ref)
    for b in range(pages_ref.shape[0]):
        out_ref[owner_ref[b]] = pages_ref[b]


def bucket_pages(owners, pages, after):
    vmem = pl.BlockSpec(memory_space=pltpu.VMEM)
    return pl.pallas_call(
        bucket_kernel,
        in_specs=[SMEM, vmem, ANY],
        out_specs=vmem,
        out_shape=jax.ShapeDtypeStruct((N_DEC,) + pages.shape[1:], pages.dtype),
        compiler_params=pltpu.CompilerParams(vmem_limit_bytes=VMEM_LIMIT),
        cost_estimate=pl.CostEstimate(flops=0, bytes_accessed=3 << 18, transcendentals=0),
    )(owners, pages, after)


def stack_kernel(a_ref, b_ref, c_ref, *rest):
    out_ref = rest[-1]
    for i, ref in enumerate((a_ref, b_ref, c_ref)):
        out_ref[i] = ref[...]


def stack_after(parts, after):
    vmem = pl.BlockSpec(memory_space=pltpu.VMEM)
    return pl.pallas_call(
        stack_kernel,
        in_specs=[vmem] * 3 + [ANY] * len(after),
        out_specs=vmem,
        out_shape=jax.ShapeDtypeStruct((3,) + parts[0].shape, parts[0].dtype),
        cost_estimate=pl.CostEstimate(flops=0, bytes_accessed=3 << 19, transcendentals=0),
    )(*parts, *after)


def place_table():
    rows = []
    for p in range(N_PRE):
        for d in range(N_DEC):
            z, y = divmod(d, N_Y)
            rows.append([p, y, z, d % 2, p * 8])
    return np.array(rows, np.int32)


def on_device(
    queries, branch_kv, pool_kv, page_lists, anc_len, dec_owner, output_projection_weight
):
    pre_idx = lax.axis_index("pre")
    dec_idx = lax.axis_index("dec")
    branch_count, page_len, cols = queries.shape
    table = jnp.asarray(place_table())
    place = lax.dynamic_index_in_dim(table, pre_idx * N_DEC + dec_idx, keepdims=False)

    both = jnp.stack([pool_kv, swap_pair(pool_kv)])
    kv = lax.all_gather(both, "pre", axis=0)
    other_own = swap_pair(branch_kv)

    sent = weight_pieces(place, output_projection_weight, pool_kv)
    received = [shift_dec(w, 0, s) for s, w in zip((1, 2, 3), sent)]
    gathered = lax.all_gather(stack_after(received, ()), "pre", axis=0)


    def attend(first, count, after=()):
        attn = attention(
            queries, branch_kv, other_own, kv, page_lists, anc_len, place, first, count, after
        ).reshape(count * page_len, cols)
        return [attn] + [shift_dec(attn, 0, s) for s in (1, 2, 3)]

    def product(attn, after=()):
        args = (place, attn, output_projection_weight, gathered, COST)
        low, high = project(True, *args, after)
        low, high_from = shift_dec(low, 1, 0), shift_dec(high, -1, 0)
        to_next, to_last, total = project(False, *args, (high,))
        to_next, to_last = relay(to_next, to_last, low, high_from)
        for part in (shift_dec(to_next, 1, 0), shift_dec(to_last, -1, 0)):
            total = total + part.astype(jnp.float32)
        return to_next, total.astype(jnp.bfloat16).reshape(-1, page_len, 512)

    one = attend(0, FIRST)
    two = attend(FIRST, branch_count - FIRST, (one[0],))
    term, out_one = product(one)

    owners = lax.dynamic_slice_in_dim(dec_owner, pre_idx * branch_count, branch_count, 0)
    buckets = bucket_pages(owners, branch_kv, two[0])
    owned = lax.all_to_all(buckets, "dec", split_axis=0, concat_axis=0, tiled=True)
    last, out_two = product(two, (term,))
    owned = copy_after(owned, last)
    moved = lax.all_to_all(owned, "pre", split_axis=0, concat_axis=0, tiled=True)

    layer_out = jnp.concatenate([out_one, out_two], axis=0)
    moved = moved.reshape(N_PRE, 2, page_len, HD).transpose(0, 2, 1, 3)
    decode_pages = moved.reshape(N_PRE, page_len, 2 * HD)
    return (layer_out, decode_pages)


def solution(mesh):
    in_specs = (
        P("pre", None, "dec"),
        P("pre", None, "dec"),
        P("pre", None, "dec"),
        P(),
        P(),
        P(),
        P("dec", None),
    )
    out_specs = (P("pre", None, "dec"), P("dec", None, "pre"))
    return jax.shard_map(
        on_device, mesh=mesh, in_specs=in_specs, out_specs=out_specs, check_vma=False
    )
```

```python
import functools

import jax
import jax.numpy as jnp
import numpy as np
from jax import lax
from jax.experimental import pallas as pl
from jax.experimental.pallas import tpu as pltpu
from jax.sharding import PartitionSpec as P

HD = 128
PAGE = 128
NANC = 16
ANCESTORS = NANC * PAGE
KEYS = ANCESTORS + PAGE
LOG2E = 1.4426950408889634
MASKED = -1e30
N_X, N_CORE, N_Z, N_Y = 4, 2, 4, 4
N_PRE, N_DEC = N_X * N_CORE, N_Z * N_Y
VMEM_LIMIT = 60 << 20
COST = 1 << 36
FIRST = 4
PRE_AT, Y_AT, Z_AT, ODD_AT, ROW_AT = range(5)
ANY = pl.BlockSpec(memory_space=pl.ANY)
SMEM = pl.BlockSpec(memory_space=pltpu.SMEM)


def shift_pre(value, dx, dcore):
    pairs = []
    for p in range(N_PRE):
        x, core = divmod(p, N_CORE)
        pairs.append((p, (x + dx) % N_X * N_CORE + (core + dcore) % N_CORE))
    return lax.ppermute(value, "pre", pairs)


def shift_dec(value, dz, dy):
    pairs = []
    for d in range(N_DEC):
        z, y = divmod(d, N_Y)
        pairs.append((d, (z + dz) % N_Z * N_Y + (y + dy) % N_Y))
    return lax.ppermute(value, "dec", pairs)


def swap_pair(value):
    return lax.ppermute(value, "dec", [(d, d ^ 1) for d in range(N_DEC)])


def dot_nt(a, b):
    return lax.dot_general(a, b, (((1,), (1,)), ((), ())), preferred_element_type=jnp.float32)


def dot_nn(a, b):
    return lax.dot_general(a, b, (((1,), (0,)), ((), ())), preferred_element_type=jnp.float32)


def attention_kernel(
    first, heads, pages_ref, len_ref, place_ref, q_ref, mine_ref, other_ref, kv_ref, *rest
):
    out_ref, kv, s_ref, k_all, v_all, sem = rest[-6:]
    odd = place_ref[ODD_AT]
    row = place_ref[ROW_AT] + first + pl.program_id(0)

    def load(slots):
        for slot in slots:
            page = pages_ref[row, slot]
            k_all[slot * PAGE : (slot + 1) * PAGE] = kv[page >> 2, odd, page & 3]
            v_all[slot * PAGE : (slot + 1) * PAGE, :HD] = kv[page >> 2, 1 - odd, page & 3]

    @pl.when(pl.program_id(0) == 0)
    def _():
        copy = pltpu.make_async_copy(kv_ref, kv, sem)
        copy.start()
        v_all[:, HD:] = jnp.ones((KEYS, HD), jnp.bfloat16)
        copy.wait()
        load(range(NANC // 2))

    load(range(NANC // 2, NANC))
    mine_is_key = odd == 0
    mine, other = mine_ref[0], other_ref[0]
    k_all[ANCESTORS:] = jnp.where(mine_is_key, mine, other)
    v_all[ANCESTORS:, :HD] = jnp.where(mine_is_key, other, mine)

    count = len_ref[row]
    scale = HD**-0.5 * LOG2E
    rows = 2 * PAGE
    for tile in range(heads // 2):
        here = slice(tile * rows, (tile + 1) * rows)
        lanes = [slice(h * HD, (h + 1) * HD) for h in (2 * tile, 2 * tile + 1)]
        q = jnp.concatenate([q_ref[0, :, cols] for cols in lanes], axis=0)
        token = lax.broadcasted_iota(jnp.int32, (2, PAGE, PAGE), 1).reshape(rows, PAGE)
        key = lax.broadcasted_iota(jnp.int32, (rows, PAGE), 1)
        own = jnp.where(key <= token, dot_nt(q, k_all[ANCESTORS:]), MASKED)
        peak = own
        for low in range(0, ANCESTORS, 256):
            s = dot_nt(q, k_all[low : low + 256])
            if low >= ANCESTORS // 2:
                position = lax.broadcasted_iota(jnp.int32, (1, 256), 1) + low
                s = s + jnp.where(position < count, 0.0, MASKED)
            s_ref[here, low : low + 256] = s
            peak = jnp.maximum(peak, jnp.maximum(s[:, :128], s[:, 128:]))
        peak = jnp.max(peak, axis=1, keepdims=True) * scale
        probs = [
            jnp.exp2(s_ref[here, low : low + 256] * scale - peak).astype(jnp.bfloat16)
            for low in range(0, ANCESTORS, 256)
        ]
        probs.append(jnp.exp2(own * scale - peak).astype(jnp.bfloat16))
        acc = dot_nn(jnp.concatenate(probs, axis=1), v_all[...])
        out = (acc[:, :HD] / acc[:, HD:]).astype(out_ref.dtype)
        for i, cols in enumerate(lanes):
            out_ref[0, :, cols] = out[i * PAGE : (i + 1) * PAGE]


def attention(q, mine, other, kv, pages, lens, place, first, count, after=()):
    cols = q.shape[2]
    heads = cols // HD
    grid_spec = pltpu.PrefetchScalarGridSpec(
        num_scalar_prefetch=3,
        grid=(count,),
        in_specs=[
            pl.BlockSpec((1, PAGE, cols), lambda b, *_: (first + b, 0, 0)),
            pl.BlockSpec((1, PAGE, HD), lambda b, *_: (first + b, 0, 0)),
            pl.BlockSpec((1, PAGE, HD), lambda b, *_: (first + b, 0, 0)),
        ]
        + [ANY] * (1 + len(after)),
        out_specs=pl.BlockSpec((1, PAGE, cols), lambda b, *_: (b, 0, 0)),
        scratch_shapes=[
            pltpu.VMEM((N_PRE, 2, 4, PAGE, HD), jnp.bfloat16),
            pltpu.VMEM((heads * PAGE, ANCESTORS), jnp.float32),
            pltpu.VMEM((KEYS, HD), jnp.bfloat16),
            pltpu.VMEM((KEYS, 2 * HD), jnp.bfloat16),
            pltpu.SemaphoreType.DMA,
        ],
    )
    work = count * heads * PAGE * KEYS
    return pl.pallas_call(
        functools.partial(attention_kernel, first, heads),
        grid_spec=grid_spec,
        out_shape=jax.ShapeDtypeStruct((count, PAGE, cols), jnp.bfloat16),
        compiler_params=pltpu.CompilerParams(vmem_limit_bytes=24 << 20),
        cost_estimate=pl.CostEstimate(
            flops=work * 128 * 4 * 2, bytes_accessed=4 << 20, transcendentals=work
        ),
    )(pages, lens, place, q, mine, other, kv, *after)


def weight_pieces_kernel(place_ref, w_ref, _, one_ref, two_ref, three_ref, sems):
    pre, y = place_ref[PRE_AT], place_ref[Y_AT]
    copies = []
    for s, out_ref in ((1, one_ref), (2, two_ref), (3, three_ref)):
        col = lax.rem(y + s, N_Y)
        for z in range(N_Z):
            copies.append(
                pltpu.make_async_copy(
                    w_ref.at[pl.ds(pre * 64, 64), pl.ds((z * N_Y + col) * 512, 512)],
                    out_ref.at[z],
                    sems.at[s - 1, z],
                )
            )
    for copy in copies:
        copy.start()
    for copy in copies:
        copy.wait()


def weight_pieces(place, weight, after):
    shape = jax.ShapeDtypeStruct((N_Z, 64, 512), jnp.bfloat16)
    return pl.pallas_call(
        weight_pieces_kernel,
        in_specs=[SMEM, ANY, ANY],
        out_specs=[pl.BlockSpec(memory_space=pltpu.VMEM)] * 3,
        out_shape=[shape] * 3,
        scratch_shapes=[pltpu.SemaphoreType.DMA((3, N_Z))],
        compiler_params=pltpu.CompilerParams(vmem_limit_bytes=VMEM_LIMIT),
        cost_estimate=pl.CostEstimate(flops=0, bytes_accessed=3 << 19, transcendentals=0),
    )(place, weight, after)


def project_body(steps, place_ref, a0, a1, a2, a3, w0, w1, w2, w3, *rest):
    acc = dot_nn(a0[...], w0[...])
    for a, w in ((a1, w1), (a2, w2), (a3, w3)):
        acc = acc + dot_nn(a[...], w[...].reshape(512, 512))
    for step, out in enumerate(rest[-steps:]):

        @pl.when(pl.program_id(0) == step)
        def _():
            out[...] = acc.astype(out.dtype)


def project(far, place, attn, weight, gathered, cost, after=()):
    rows = attn[0].shape[0] // (2 if far else 1)
    steps = 2 if far else 3

    def column(i, w):
        return lax.rem(w[Z_AT] + (2 if far else 1 + i + jnp.minimum(i, 1)), N_Z)

    def here(i, w):
        return (i if far else 0, 0)

    out = pl.BlockSpec((rows, 512), lambda i, w: (0, 0))
    grid_spec = pltpu.PrefetchScalarGridSpec(
        num_scalar_prefetch=1,
        grid=(steps,),
        in_specs=[pl.BlockSpec((rows, 512), here)] * 4
        + [pl.BlockSpec((512, 512), lambda i, w: (0, column(i, w) * N_Y + w[Y_AT]))]
        + [
            pl.BlockSpec((N_PRE, 1, 1, 64, 512), lambda i, w, s=s: (0, s, column(i, w), 0, 0))
            for s in range(3)
        ]
        + [ANY] * len(after),
        out_specs=[out] * steps,
        scratch_shapes=[],
    )
    kinds = [jnp.bfloat16] * 2 + [jnp.float32] * (steps - 2)
    return pl.pallas_call(
        functools.partial(project_body, steps),
        grid_spec=grid_spec,
        out_shape=[jax.ShapeDtypeStruct((rows, 512), kind) for kind in kinds],
        compiler_params=pltpu.CompilerParams(vmem_limit_bytes=VMEM_LIMIT),
        cost_estimate=pl.CostEstimate(flops=cost, bytes_accessed=cost >> 4, transcendentals=0),
    )(place, *attn, weight, gathered, gathered, gathered, *after)


def relay_kernel(next_ref, last_ref, low_ref, high_ref, next_out, last_out):
    half = low_ref.shape[0]
    up = next_ref[:half].astype(jnp.float32) + low_ref[...].astype(jnp.float32)
    next_out[:half] = up.astype(jnp.bfloat16)
    next_out[half:] = next_ref[half:]
    down = last_ref[half:].astype(jnp.float32) + high_ref[...].astype(jnp.float32)
    last_out[half:] = down.astype(jnp.bfloat16)
    last_out[:half] = last_ref[:half]


def relay(to_next, to_last, low, high):
    vmem = pl.BlockSpec(memory_space=pltpu.VMEM)
    return pl.pallas_call(
        relay_kernel,
        in_specs=[vmem] * 4,
        out_specs=[vmem] * 2,
        out_shape=[jax.ShapeDtypeStruct(to_next.shape, to_next.dtype)] * 2,
        cost_estimate=pl.CostEstimate(flops=1 << 20, bytes_accessed=3 << 20, transcendentals=0),
    )(to_next, to_last, low, high)


def bucket_kernel(owner_ref, pages_ref, _, out_ref):
    out_ref[...] = jnp.zeros_like(out_ref)
    for b in range(pages_ref.shape[0]):
        out_ref[owner_ref[b]] = pages_ref[b]


def bucket_pages(owners, pages, after):
    vmem = pl.BlockSpec(memory_space=pltpu.VMEM)
    return pl.pallas_call(
        bucket_kernel,
        in_specs=[SMEM, vmem, ANY],
        out_specs=vmem,
        out_shape=jax.ShapeDtypeStruct((N_DEC,) + pages.shape[1:], pages.dtype),
        compiler_params=pltpu.CompilerParams(vmem_limit_bytes=VMEM_LIMIT),
        cost_estimate=pl.CostEstimate(flops=0, bytes_accessed=3 << 18, transcendentals=0),
    )(owners, pages, after)


def stack_kernel(a_ref, b_ref, c_ref, *rest):
    out_ref = rest[-1]
    for i, ref in enumerate((a_ref, b_ref, c_ref)):
        out_ref[i] = ref[...]


def stack_after(parts, after):
    vmem = pl.BlockSpec(memory_space=pltpu.VMEM)
    return pl.pallas_call(
        stack_kernel,
        in_specs=[vmem] * 3 + [ANY] * len(after),
        out_specs=vmem,
        out_shape=jax.ShapeDtypeStruct((3,) + parts[0].shape, parts[0].dtype),
        cost_estimate=pl.CostEstimate(flops=0, bytes_accessed=3 << 19, transcendentals=0),
    )(*parts, *after)


def place_table():
    rows = []
    for p in range(N_PRE):
        for d in range(N_DEC):
            z, y = divmod(d, N_Y)
            rows.append([p, y, z, d % 2, p * 8])
    return np.array(rows, np.int32)


def on_device(
    queries, branch_kv, pool_kv, page_lists, anc_len, dec_owner, output_projection_weight
):
    pre_idx = lax.axis_index("pre")
    dec_idx = lax.axis_index("dec")
    branch_count, page_len, cols = queries.shape
    table = jnp.asarray(place_table())
    place = lax.dynamic_index_in_dim(table, pre_idx * N_DEC + dec_idx, keepdims=False)

    both = jnp.stack([pool_kv, swap_pair(pool_kv)])
    kv = lax.all_gather(both, "pre", axis=0)
    other_own = swap_pair(branch_kv)

    sent = weight_pieces(place, output_projection_weight, pool_kv)
    received = [shift_dec(w, 0, s) for s, w in zip((1, 2, 3), sent)]

    owners = lax.dynamic_slice_in_dim(dec_owner, pre_idx * branch_count, branch_count, 0)
    buckets = bucket_pages(owners, branch_kv, sent[0])
    owned = lax.all_to_all(buckets, "dec", split_axis=0, concat_axis=0, tiled=True)
    moved = lax.all_to_all(owned, "pre", split_axis=0, concat_axis=0, tiled=True)

    gathered = lax.all_gather(stack_after(received, (other_own,)), "pre", axis=0)


    def attend(first, count, after=()):
        attn = attention(
            queries, branch_kv, other_own, kv, page_lists, anc_len, place, first, count, after
        ).reshape(count * page_len, cols)
        return [attn] + [shift_dec(attn, 0, s) for s in (1, 2, 3)]

    def product(attn, after=()):
        args = (place, attn, output_projection_weight, gathered, COST)
        low, high = project(True, *args, after)
        low, high_from = shift_dec(low, 1, 0), shift_dec(high, -1, 0)
        to_next, to_last, total = project(False, *args, (high,))
        to_next, to_last = relay(to_next, to_last, low, high_from)
        for part in (shift_dec(to_next, 1, 0), shift_dec(to_last, -1, 0)):
            total = total + part.astype(jnp.float32)
        return to_next, total.astype(jnp.bfloat16).reshape(-1, page_len, 512)

    one = attend(0, FIRST)
    two = attend(FIRST, branch_count - FIRST, (one[0], owned))
    term, out_one = product(one)
    _, out_two = product(two, (term, moved))

    layer_out = jnp.concatenate([out_one, out_two], axis=0)
    moved = moved.reshape(N_PRE, 2, page_len, HD).transpose(0, 2, 1, 3)
    decode_pages = moved.reshape(N_PRE, page_len, 2 * HD)
    return (layer_out, decode_pages)


def solution(mesh):
    in_specs = (
        P("pre", None, "dec"),
        P("pre", None, "dec"),
        P("pre", None, "dec"),
        P(),
        P(),
        P(),
        P("dec", None),
    )
    out_specs = (P("pre", None, "dec"), P("dec", None, "pre"))
    return jax.shard_map(
        on_device, mesh=mesh, in_specs=in_specs, out_specs=out_specs, check_vma=False
    )
```

```python
import functools

import jax
import jax.numpy as jnp
import numpy as np
from jax import lax
from jax.experimental import pallas as pl
from jax.experimental.pallas import tpu as pltpu
from jax.sharding import PartitionSpec as P

HD = 128
PAGE = 128
NANC = 16
ANCESTORS = NANC * PAGE
KEYS = ANCESTORS + PAGE
LOG2E = 1.4426950408889634
MASKED = -1e30
N_X, N_CORE, N_Z, N_Y = 4, 2, 4, 4
N_PRE, N_DEC = N_X * N_CORE, N_Z * N_Y
VMEM_LIMIT = 60 << 20
COST = 1 << 36
FIRST = 4
PRE_AT, Y_AT, Z_AT, ODD_AT, ROW_AT = range(5)
ANY = pl.BlockSpec(memory_space=pl.ANY)
SMEM = pl.BlockSpec(memory_space=pltpu.SMEM)


def shift_pre(value, dx, dcore):
    pairs = []
    for p in range(N_PRE):
        x, core = divmod(p, N_CORE)
        pairs.append((p, (x + dx) % N_X * N_CORE + (core + dcore) % N_CORE))
    return lax.ppermute(value, "pre", pairs)


def shift_dec(value, dz, dy):
    pairs = []
    for d in range(N_DEC):
        z, y = divmod(d, N_Y)
        pairs.append((d, (z + dz) % N_Z * N_Y + (y + dy) % N_Y))
    return lax.ppermute(value, "dec", pairs)


def swap_pair(value):
    return lax.ppermute(value, "dec", [(d, d ^ 1) for d in range(N_DEC)])


def dot_nt(a, b):
    return lax.dot_general(a, b, (((1,), (1,)), ((), ())), preferred_element_type=jnp.float32)


def dot_nn(a, b):
    return lax.dot_general(a, b, (((1,), (0,)), ((), ())), preferred_element_type=jnp.float32)


def attention_kernel(
    first, heads, pages_ref, len_ref, place_ref, q_ref, mine_ref, other_ref, kv_ref, *rest
):
    out_ref, kv, s_ref, k_all, v_all, sem = rest[-6:]
    odd = place_ref[ODD_AT]
    row = place_ref[ROW_AT] + first + pl.program_id(0)

    def load(slots):
        for slot in slots:
            page = pages_ref[row, slot]
            k_all[slot * PAGE : (slot + 1) * PAGE] = kv[page >> 2, odd, page & 3]
            v_all[slot * PAGE : (slot + 1) * PAGE, :HD] = kv[page >> 2, 1 - odd, page & 3]

    @pl.when(pl.program_id(0) == 0)
    def _():
        copy = pltpu.make_async_copy(kv_ref, kv, sem)
        copy.start()
        v_all[:, HD:] = jnp.ones((KEYS, HD), jnp.bfloat16)
        copy.wait()
        load(range(NANC // 2))

    load(range(NANC // 2, NANC))
    mine_is_key = odd == 0
    mine, other = mine_ref[0], other_ref[0]
    k_all[ANCESTORS:] = jnp.where(mine_is_key, mine, other)
    v_all[ANCESTORS:, :HD] = jnp.where(mine_is_key, other, mine)

    count = len_ref[row]
    scale = HD**-0.5 * LOG2E
    rows = 2 * PAGE
    for tile in range(heads // 2):
        here = slice(tile * rows, (tile + 1) * rows)
        lanes = [slice(h * HD, (h + 1) * HD) for h in (2 * tile, 2 * tile + 1)]
        q = jnp.concatenate([q_ref[0, :, cols] for cols in lanes], axis=0)
        token = lax.broadcasted_iota(jnp.int32, (2, PAGE, PAGE), 1).reshape(rows, PAGE)
        key = lax.broadcasted_iota(jnp.int32, (rows, PAGE), 1)
        own = jnp.where(key <= token, dot_nt(q, k_all[ANCESTORS:]), MASKED)
        peak = own
        for low in range(0, ANCESTORS, 256):
            s = dot_nt(q, k_all[low : low + 256])
            if low >= ANCESTORS // 2:
                position = lax.broadcasted_iota(jnp.int32, (1, 256), 1) + low
                s = s + jnp.where(position < count, 0.0, MASKED)
            s_ref[here, low : low + 256] = s
            peak = jnp.maximum(peak, jnp.maximum(s[:, :128], s[:, 128:]))
        peak = jnp.max(peak, axis=1, keepdims=True) * scale
        probs = [
            jnp.exp2(s_ref[here, low : low + 256] * scale - peak).astype(jnp.bfloat16)
            for low in range(0, ANCESTORS, 256)
        ]
        probs.append(jnp.exp2(own * scale - peak).astype(jnp.bfloat16))
        acc = dot_nn(jnp.concatenate(probs, axis=1), v_all[...])
        out = (acc[:, :HD] / acc[:, HD:]).astype(out_ref.dtype)
        for i, cols in enumerate(lanes):
            out_ref[0, :, cols] = out[i * PAGE : (i + 1) * PAGE]


def attention(q, mine, other, kv, pages, lens, place, first, count, after=()):
    cols = q.shape[2]
    heads = cols // HD
    grid_spec = pltpu.PrefetchScalarGridSpec(
        num_scalar_prefetch=3,
        grid=(count,),
        in_specs=[
            pl.BlockSpec((1, PAGE, cols), lambda b, *_: (first + b, 0, 0)),
            pl.BlockSpec((1, PAGE, HD), lambda b, *_: (first + b, 0, 0)),
            pl.BlockSpec((1, PAGE, HD), lambda b, *_: (first + b, 0, 0)),
        ]
        + [ANY] * (1 + len(after)),
        out_specs=pl.BlockSpec((1, PAGE, cols), lambda b, *_: (b, 0, 0)),
        scratch_shapes=[
            pltpu.VMEM((N_PRE, 2, 4, PAGE, HD), jnp.bfloat16),
            pltpu.VMEM((heads * PAGE, ANCESTORS), jnp.float32),
            pltpu.VMEM((KEYS, HD), jnp.bfloat16),
            pltpu.VMEM((KEYS, 2 * HD), jnp.bfloat16),
            pltpu.SemaphoreType.DMA,
        ],
    )
    work = count * heads * PAGE * KEYS
    return pl.pallas_call(
        functools.partial(attention_kernel, first, heads),
        grid_spec=grid_spec,
        out_shape=jax.ShapeDtypeStruct((count, PAGE, cols), jnp.bfloat16),
        compiler_params=pltpu.CompilerParams(vmem_limit_bytes=24 << 20),
        cost_estimate=pl.CostEstimate(
            flops=work * 128 * 4 * 2, bytes_accessed=4 << 20, transcendentals=work
        ),
    )(pages, lens, place, q, mine, other, kv, *after)


def weight_pieces_kernel(place_ref, w_ref, _, one_ref, two_ref, three_ref, sems):
    pre, y = place_ref[PRE_AT], place_ref[Y_AT]
    copies = []
    for s, out_ref in ((1, one_ref), (2, two_ref), (3, three_ref)):
        col = lax.rem(y + s, N_Y)
        for z in range(N_Z):
            copies.append(
                pltpu.make_async_copy(
                    w_ref.at[pl.ds(pre * 64, 64), pl.ds((z * N_Y + col) * 512, 512)],
                    out_ref.at[z],
                    sems.at[s - 1, z],
                )
            )
    for copy in copies:
        copy.start()
    for copy in copies:
        copy.wait()


def weight_pieces(place, weight, after):
    shape = jax.ShapeDtypeStruct((N_Z, 64, 512), jnp.bfloat16)
    return pl.pallas_call(
        weight_pieces_kernel,
        in_specs=[SMEM, ANY, ANY],
        out_specs=[pl.BlockSpec(memory_space=pltpu.VMEM)] * 3,
        out_shape=[shape] * 3,
        scratch_shapes=[pltpu.SemaphoreType.DMA((3, N_Z))],
        compiler_params=pltpu.CompilerParams(vmem_limit_bytes=VMEM_LIMIT),
        cost_estimate=pl.CostEstimate(flops=0, bytes_accessed=3 << 19, transcendentals=0),
    )(place, weight, after)


def project_body(steps, place_ref, a0, a1, a2, a3, w0, w1, w2, w3, *rest):
    acc = dot_nn(a0[...], w0[...])
    for a, w in ((a1, w1), (a2, w2), (a3, w3)):
        acc = acc + dot_nn(a[...], w[...].reshape(512, 512))
    for step, out in enumerate(rest[-steps:]):

        @pl.when(pl.program_id(0) == step)
        def _():
            out[...] = acc.astype(out.dtype)


def project(far, place, attn, weight, gathered, cost, after=()):
    rows = attn[0].shape[0] // (2 if far else 1)
    steps = 2 if far else 3

    def column(i, w):
        return lax.rem(w[Z_AT] + (2 if far else 1 + i + jnp.minimum(i, 1)), N_Z)

    def here(i, w):
        return (i if far else 0, 0)

    out = pl.BlockSpec((rows, 512), lambda i, w: (0, 0))
    grid_spec = pltpu.PrefetchScalarGridSpec(
        num_scalar_prefetch=1,
        grid=(steps,),
        in_specs=[pl.BlockSpec((rows, 512), here)] * 4
        + [pl.BlockSpec((512, 512), lambda i, w: (0, column(i, w) * N_Y + w[Y_AT]))]
        + [
            pl.BlockSpec((N_PRE, 1, 1, 64, 512), lambda i, w, s=s: (0, s, column(i, w), 0, 0))
            for s in range(3)
        ]
        + [ANY] * len(after),
        out_specs=[out] * steps,
        scratch_shapes=[],
    )
    kinds = [jnp.bfloat16] * 2 + [jnp.float32] * (steps - 2)
    return pl.pallas_call(
        functools.partial(project_body, steps),
        grid_spec=grid_spec,
        out_shape=[jax.ShapeDtypeStruct((rows, 512), kind) for kind in kinds],
        compiler_params=pltpu.CompilerParams(vmem_limit_bytes=48 << 20),
        cost_estimate=pl.CostEstimate(flops=cost, bytes_accessed=cost >> 4, transcendentals=0),
    )(place, *attn, weight, gathered, gathered, gathered, *after)


def relay_kernel(next_ref, last_ref, low_ref, high_ref, next_out, last_out):
    half = low_ref.shape[0]
    up = next_ref[:half].astype(jnp.float32) + low_ref[...].astype(jnp.float32)
    next_out[:half] = up.astype(jnp.bfloat16)
    next_out[half:] = next_ref[half:]
    down = last_ref[half:].astype(jnp.float32) + high_ref[...].astype(jnp.float32)
    last_out[half:] = down.astype(jnp.bfloat16)
    last_out[:half] = last_ref[:half]


def relay(to_next, to_last, low, high):
    vmem = pl.BlockSpec(memory_space=pltpu.VMEM)
    return pl.pallas_call(
        relay_kernel,
        in_specs=[vmem] * 4,
        out_specs=[vmem] * 2,
        out_shape=[jax.ShapeDtypeStruct(to_next.shape, to_next.dtype)] * 2,
        cost_estimate=pl.CostEstimate(flops=1 << 20, bytes_accessed=3 << 20, transcendentals=0),
    )(to_next, to_last, low, high)


def bucket_kernel(owner_ref, pages_ref, _, out_ref):
    out_ref[...] = jnp.zeros_like(out_ref)
    for b in range(pages_ref.shape[0]):
        out_ref[owner_ref[b]] = pages_ref[b]


def bucket_pages(owners, pages, after):
    vmem = pl.BlockSpec(memory_space=pltpu.VMEM)
    return pl.pallas_call(
        bucket_kernel,
        in_specs=[SMEM, vmem, ANY],
        out_specs=vmem,
        out_shape=jax.ShapeDtypeStruct((N_DEC,) + pages.shape[1:], pages.dtype),
        compiler_params=pltpu.CompilerParams(vmem_limit_bytes=VMEM_LIMIT),
        cost_estimate=pl.CostEstimate(flops=0, bytes_accessed=3 << 18, transcendentals=0),
    )(owners, pages, after)


def stack_kernel(a_ref, b_ref, c_ref, *rest):
    out_ref = rest[-1]
    for i, ref in enumerate((a_ref, b_ref, c_ref)):
        out_ref[i] = ref[...]


def stack_after(parts, after):
    vmem = pl.BlockSpec(memory_space=pltpu.VMEM)
    return pl.pallas_call(
        stack_kernel,
        in_specs=[vmem] * 3 + [ANY] * len(after),
        out_specs=vmem,
        out_shape=jax.ShapeDtypeStruct((3,) + parts[0].shape, parts[0].dtype),
        cost_estimate=pl.CostEstimate(flops=0, bytes_accessed=3 << 19, transcendentals=0),
    )(*parts, *after)


def place_table():
    rows = []
    for p in range(N_PRE):
        for d in range(N_DEC):
            z, y = divmod(d, N_Y)
            rows.append([p, y, z, d % 2, p * 8])
    return np.array(rows, np.int32)


def on_device(
    queries, branch_kv, pool_kv, page_lists, anc_len, dec_owner, output_projection_weight
):
    pre_idx = lax.axis_index("pre")
    dec_idx = lax.axis_index("dec")
    branch_count, page_len, cols = queries.shape
    table = jnp.asarray(place_table())
    place = lax.dynamic_index_in_dim(table, pre_idx * N_DEC + dec_idx, keepdims=False)

    both = jnp.stack([pool_kv, swap_pair(pool_kv)])
    kv = lax.all_gather(both, "pre", axis=0)
    other_own = swap_pair(branch_kv)

    sent = weight_pieces(place, output_projection_weight, pool_kv)
    received = [shift_dec(w, 0, s) for s, w in zip((1, 2, 3), sent)]

    owners = lax.dynamic_slice_in_dim(dec_owner, pre_idx * branch_count, branch_count, 0)
    buckets = bucket_pages(owners, branch_kv, sent[0])
    owned = lax.all_to_all(buckets, "dec", split_axis=0, concat_axis=0, tiled=True)
    moved = lax.all_to_all(owned, "pre", split_axis=0, concat_axis=0, tiled=True)

    gathered = lax.all_gather(stack_after(received, (other_own,)), "pre", axis=0)


    def attend(first, count, after=()):
        attn = attention(
            queries, branch_kv, other_own, kv, page_lists, anc_len, place, first, count, after
        ).reshape(count * page_len, cols)
        return [attn] + [shift_dec(attn, 0, s) for s in (1, 2, 3)]

    def product(attn, after=()):
        args = (place, attn, output_projection_weight, gathered, COST)
        low, high = project(True, *args, after)
        low, high_from = shift_dec(low, 1, 0), shift_dec(high, -1, 0)
        to_next, to_last, total = project(False, *args, (high,))
        to_next, to_last = relay(to_next, to_last, low, high_from)
        for part in (shift_dec(to_next, 1, 0), shift_dec(to_last, -1, 0)):
            total = total + part.astype(jnp.float32)
        return to_next, total.astype(jnp.bfloat16).reshape(-1, page_len, 512)

    one = attend(0, FIRST)
    two = attend(FIRST, branch_count - FIRST, (one[0], owned))
    term, out_one = product(one)
    _, out_two = product(two, (term, moved))

    layer_out = jnp.concatenate([out_one, out_two], axis=0)
    moved = moved.reshape(N_PRE, 2, page_len, HD).transpose(0, 2, 1, 3)
    decode_pages = moved.reshape(N_PRE, page_len, 2 * HD)
    return (layer_out, decode_pages)


def solution(mesh):
    in_specs = (
        P("pre", None, "dec"),
        P("pre", None, "dec"),
        P("pre", None, "dec"),
        P(),
        P(),
        P(),
        P("dec", None),
    )
    out_specs = (P("pre", None, "dec"), P("dec", None, "pre"))
    return jax.shard_map(
        on_device, mesh=mesh, in_specs=in_specs, out_specs=out_specs, check_vma=False
    )
```
